512 devices in a mesh: row: 32 (over y, x), col: 16 (over z, core).
Axes of the slice: x: 4, y: 8, z: 8, core: 2. Of those that a mesh axis runs over, the one named last changes fastest.
Arguments:
- density: bfloat16 [384, 32, 128, 128], P('row', 'col'), may hold values from -0.6 to 0.6, as said below
- density_pattern: int32 [384, 32], P('row', 'col'), may hold values from 0 to 1, as said below
- filter_pattern: int32 [384, 32], P('row', 'col'), may hold values from 0 to 1, as said below
Outputs:
- purified: bfloat16 [384, 32, 128, 128], P('row', 'col')
The draws below stay inside these ranges and needn't reach their ends.
Inputs may be any that keep to these rules, and one draw needn't show every extreme that they name: `density`: the tiles form a symmetric matrix: the tile of block row i at block column j is the transpose of the tile of block row j at block column i, and each diagonal tile is symmetric. `density_pattern`: 1 marks a tile of the pattern. With n = 16, slot s = c * 2 + q of block row i stands for block column (i + d) mod 384, d = -8 + ((c - i + 8) mod n) + q * n; a slot with d > 8 is always 0, the slot with d = 0 is always 1, and the pattern is symmetric: (i, j) is marked exactly when (j, i) is. `filter_pattern`: 1 marks a tile kept in the filtered products, with the slots as for density_pattern; a slot with d > 8 is always 0, the slot with d = 0 is always 1, and the pattern is symmetric.
All inputs are finite; a program needn't handle non-finite values.
Results may differ from the reference program's by a relative error of at most 0.0041.
Values may be sent and summed in bfloat16 or wider, within the bound.
No kernel may reach another device: no remote copies, remote signals or barrier semaphores. Data moves between devices by JAX's collectives and lax.ppermute only.
A program may use at most 128 MiB of HBM per device.

```python
import jax
import jax.numpy as jnp
from jax import lax

BS = 128
W = 8
K = 2
SLOTS = 32
NB = 384


def slot_form(offsets):
    groups = SLOTS // K
    row_ids = jnp.arange(NB, dtype=jnp.int32)[:, None]
    slot_ids = jnp.arange(SLOTS, dtype=jnp.int32)[None, :]
    reach = jnp.mod(slot_ids // K - row_ids + W, groups) + slot_ids % K * groups
    inside = reach <= 2 * W
    picks = jnp.minimum(reach, 2 * W).astype(jnp.int32)
    picked = jax.vmap(lambda block_row, chosen: block_row[chosen])(offsets, picks)
    shaped = inside.reshape(inside.shape + (1,) * (offsets.ndim - 2))
    return jnp.where(shaped, picked, jnp.zeros((), offsets.dtype))


def mirror_band(upper, flip):
    row_ids = jnp.arange(NB, dtype=jnp.int32)
    lower = []
    for step in range(W, 0, -1):
        source = jnp.mod(row_ids - step, NB).astype(jnp.int32)
        taken = upper[source, step]
        if flip:
            taken = jnp.swapaxes(taken, -1, -2)
        lower.append(taken)
    return jnp.stack(lower + [upper[:, index] for index in range(W + 1)], axis=1)


def band_pattern(key, chance):
    ticket = jax.random.randint(key, (NB, W + 1), 0, 20)
    reach = jnp.arange(W + 1, dtype=jnp.int32)[None, :]
    upper = jnp.where((ticket < chance) | (reach == 0), 1, 0).astype(jnp.int32)
    return slot_form(mirror_band(upper, False)).astype(jnp.int32)


def draw_density(key, part):
    key = jax.random.fold_in(key, 5)
    raw = 0.1 * jax.random.normal(key, (NB, W + 1, BS, BS), jnp.float32)
    centre = (raw[:, 0] + jnp.swapaxes(raw[:, 0], -1, -2)) * 0.7071
    raw = raw.at[:, 0].set(centre)
    raw = jnp.clip(raw, -0.59, 0.59)
    return slot_form(mirror_band(raw, True)).astype(jnp.bfloat16)


def draw_density_pattern(key, part):
    key = jax.random.fold_in(key, 11)
    return band_pattern(key, 17)


def draw_filter_pattern(key, part):
    key = jax.random.fold_in(key, 23)
    return band_pattern(key, 15)


def setup_inputs(seed: int = 0) -> dict:
    key_of = jax.random.split(jax.random.key(seed), 4)
    density = draw_density(jax.random.fold_in(key_of[3], 71), 0)
    density_pattern = draw_density_pattern(jax.random.fold_in(key_of[3], 71), 0)
    filter_pattern = draw_filter_pattern(jax.random.fold_in(key_of[3], 71), 0)
    return dict(density=density, density_pattern=density_pattern, filter_pattern=filter_pattern)


def to_offsets(blocks):
    groups = SLOTS // K
    row_ids = jnp.arange(NB, dtype=jnp.int32)[:, None]
    reach = jnp.arange(2 * W + 1, dtype=jnp.int32)[None, :]
    index = (jnp.mod(row_ids + reach - W, groups) * K + reach // groups).astype(jnp.int32)
    return jax.vmap(lambda block_row, picks: block_row[picks])(blocks, index)


def to_slots(offsets):
    groups = SLOTS // K
    row_ids = jnp.arange(NB, dtype=jnp.int32)[:, None]
    slot_ids = jnp.arange(SLOTS, dtype=jnp.int32)[None, :]
    reach = jnp.mod(slot_ids // K - row_ids + W, groups) + (slot_ids % K) * groups
    inside = reach <= 2 * W
    picks = jnp.minimum(reach, 2 * W).astype(jnp.int32)
    picked = jax.vmap(lambda block_row, chosen: block_row[chosen])(offsets, picks)
    return jnp.where(inside[:, :, None, None], picked, jnp.zeros((), offsets.dtype))


def multiply(left, right):
    reach = jnp.arange(2 * W + 1, dtype=jnp.int32)
    shifted = reach[None, :] - reach[:, None] + W
    inside = (shifted >= 0) & (shifted <= 2 * W)
    clipped = jnp.clip(shifted, 0, 2 * W).astype(jnp.int32)

    def one_row(row_number):
        sources = jnp.mod(row_number + reach - W, NB).astype(jnp.int32)
        gathered = right[sources]
        chosen = jax.vmap(lambda block_row, picks: block_row[picks])(gathered, clipped)
        chosen = jnp.where(inside[:, :, None, None], chosen.astype(jnp.float32), jnp.zeros((), jnp.float32))
        return jnp.einsum("dab,debc->eac", left[row_number].astype(jnp.float32), chosen, precision=lax.Precision.HIGHEST)

    return lax.map(one_row, jnp.arange(NB, dtype=jnp.int32))


def reference(density, density_pattern, filter_pattern):
    masked = jnp.where((density_pattern == 1)[:, :, None, None], density, jnp.zeros((), density.dtype))
    keeping = (filter_pattern == 1)[:, :, None, None]
    base = to_offsets(masked)
    square = jnp.where(keeping, to_slots(multiply(base, base)), jnp.zeros((), jnp.float32)).astype(jnp.bfloat16)
    cubic = jnp.where(keeping, to_slots(multiply(to_offsets(square), base)), jnp.zeros((), jnp.float32))
    return (3.0 * square.astype(jnp.float32) - 2.0 * cubic).astype(jnp.bfloat16)
```

```python
import functools

import jax
import jax.numpy as jnp
import numpy as np
from jax import lax
from jax.experimental import pallas as pl
from jax.experimental.pallas import tpu as pltpu
from jax.sharding import PartitionSpec as P

W = 8
EARLY = 8
LATE = 6


def assign(rows, groups):
    size = rows + 2 * W
    items = [(u, v) for u in range(size) for v in range(u, min(size, u + W + 1))]

    def seats(pair):
        found = []
        for w, j in dict.fromkeys((pair, pair[::-1])):
            kind = 0 if W <= w < W + rows else 1
            found.append(((j % groups, kind), (w, j)))
        return sorted(found)

    room = {0: EARLY, 1: LATE}
    taken = {(m, kind): [] for m in range(groups) for kind in (0, 1)}

    def place(pair, seen):
        for seat, tile in seats(pair):
            if seat in seen:
                continue
            seen.add(seat)
            if len(taken[seat]) < room[seat[1]]:
                taken[seat].append((pair, tile))
                return True
            for index, (other, _) in enumerate(taken[seat]):
                if place(other, seen):
                    taken[seat][index] = (pair, tile)
                    return True
        return False

    for pair in items:
        if not place(pair, set()):
            raise ValueError("no room")
    early = [sorted(tile for _, tile in taken[m, 0]) for m in range(groups)]
    late = [sorted(tile for _, tile in taken[m, 1]) for m in range(groups)]
    return early, late


def slot_of(w, j, first):
    return (w - first) * 2 + (1 if j - w == W else 0)


def tables(early, late, rows, groups):
    out = np.full((groups, EARLY + 2 * LATE), -1, np.int32)
    for m in range(groups):
        for e, (w, j) in enumerate(early[m]):
            out[m, e] = slot_of(w, j, W)
        for e, (w, j) in enumerate(late[m]):
            if w < W:
                out[m, EARLY + e] = slot_of(w, j, W - rows)
            else:
                out[m, EARLY + LATE + e] = slot_of(w, j, W + rows)
    return out.reshape(-1)


def relative(row_index, col_index, rows, groups):
    return lax.rem(col_index - row_index * rows + W + groups * rows * 64, groups)


def pack_kernel(rows, groups, table, pattern, keep, density, early, up, down):
    size = density.shape[-1]
    width = EARLY + 2 * LATE
    r = lax.axis_index("row")
    c = lax.axis_index("col")
    own = relative(r, c, rows, groups)
    after = relative(r + 1, c, rows, groups)
    before = relative(r + lax.axis_size("row") - 1, c, rows, groups)

    def move(target, e, slot):
        safe = jnp.maximum(slot, 0)
        used = (slot >= 0) & (pattern[safe // 2, lax.rem(safe, 2)] == 1)
        tile = density[safe]
        target[pl.ds(e * size, size), :] = jnp.where(used, tile, jnp.zeros_like(tile))

    for e in range(EARLY):
        move(early, e, table[own * width + e])
    for e in range(LATE):
        move(up, e, table[after * width + EARLY + e])
        move(down, e, table[before * width + EARLY + LATE + e])
    flags = jnp.zeros((32, size), jnp.float32)
    line = lax.broadcasted_iota(jnp.int32, (32, size), 0)
    for a in range(rows):
        for q in range(2):
            value = jnp.where(keep[a, q] == 1, 1.0, 0.0)
            flags = jnp.where(line == a * 2 + q, value, flags)
    early[pl.ds(EARLY * size, 32), :] = flags.astype(jnp.bfloat16)


def multiply_kernel(rows, groups, early_tiles, late_tiles, keep, gathered, out, dense, square, columns, flags):
    size = out.shape[-1]
    window = rows + 2 * W
    r = lax.axis_index("row")
    c = lax.axis_index("col")
    m = relative(r, c, rows, groups)
    turn = lax.rem(c - m + groups, groups)
    pair = 2 * size
    half = W // 2
    supers = window // 2

    nothing = jnp.zeros((size, size), jnp.bfloat16)
    for u in range(window):
        for v in range(window):
            if abs(u - v) > W and abs(u // 2 - v // 2) <= half:
                dense[pl.ds(u * size, size), pl.ds(v * size, size)] = nothing
    for n in range(groups):
        p = lax.rem(turn + n, groups)
        for e, (w, j) in enumerate(early_tiles[n] + late_tiles[n]):
            line = e * size if e < len(early_tiles[n]) else (EARLY + e - len(early_tiles[n])) * size + 32
            tile = gathered[p, pl.ds(line, size), :]
            dense[pl.ds(w * size, size), pl.ds(j * size, size)] = tile
            if w != j:
                dense[pl.ds(j * size, size), pl.ds(w * size, size)] = tile.T
        flags[pl.ds(n * 32, 32), :] = gathered[p, pl.ds(EARLY * size, 32), :].astype(jnp.float32)

    first = pl.multiple_of(m * size, size)
    second = pl.multiple_of(jnp.minimum(m + groups, window - 1) * size, size)
    columns[...] = jnp.zeros_like(columns)
    for j, start, place in ((m, first, 0), (jnp.minimum(m + groups, window - 1), second, size)):
        for u in range(window):
            inside = (u - j <= W) & (j - u <= W)

            @pl.when(inside)
            def _():
                columns[pl.ds(u * size, size), pl.ds(place, size)] = dense[pl.ds(u * size, size), pl.ds(start, size)]

    for step in range(rows // 2):
        top = half + step
        line = top * pair
        for other in range(top - half, top + half + 1):
            low = max(top, other) - half
            high = min(top, other) + half + 1
            product = jnp.dot(
                dense[pl.ds(line, pair), pl.ds(low * pair, (high - low) * pair)],
                dense[pl.ds(low * pair, (high - low) * pair), pl.ds(other * pair, pair)],
                preferred_element_type=jnp.float32,
            )
            for x in range(2):
                for y in range(2):
                    a, k = 2 * step + x, 2 * other + y
                    d = k - (a + W)
                    if abs(d) > W:
                        tile = jnp.zeros((size, size), jnp.bfloat16)
                    else:
                        flag = flags[pl.ds((k % groups) * 32 + a * 2 + (1 if d == W else 0), 1), :]
                        tile = product[x * size : (x + 1) * size, y * size : (y + 1) * size]
                        tile = jnp.where(flag > 0.5, tile, 0.0).astype(jnp.bfloat16)
                    square[pl.ds(a * size, size), pl.ds(k * size, size)] = tile
        low = (top - half) * pair
        deep = (2 * half + 1) * pair
        cubic = jnp.dot(
            square[pl.ds(step * pair, pair), pl.ds(low, deep)],
            columns[pl.ds(low, deep), :],
            preferred_element_type=jnp.float32,
        )
        for x in range(2):
            a = 2 * step + x
            upper = a <= m
            start = jnp.where(upper, first, second)
            start = pl.multiple_of(start, size)
            third = cubic[x * size : (x + 1) * size, :]
            chosen = jnp.where(upper, third[:, :size], third[:, size:])
            base = square[pl.ds(a * size, size), pl.ds(start, size)].astype(jnp.float32)
            value = 3.0 * base - 2.0 * chosen
            out[2 * a] = jnp.where(keep[a, 0] == 1, value, 0.0).astype(out.dtype)
            there = (keep[a, 1] == 1) & (a == m)
            base = square[pl.ds(a * size, size), pl.ds(second, size)].astype(jnp.float32)
            value = 3.0 * base - 2.0 * third[:, size:]
            out[2 * a + 1] = jnp.where(there, value, 0.0).astype(out.dtype)


def per_device(density, density_pattern, filter_pattern):
    rows, slots, size, _ = density.shape
    groups = lax.axis_size("col")
    count = lax.axis_size("row")
    early_tiles, late_tiles = assign(rows, groups)
    table = jnp.asarray(tables(early_tiles, late_tiles, rows, groups))
    window = rows + 2 * W
    smem = pl.BlockSpec(memory_space=pltpu.SMEM)
    vmem = pl.BlockSpec(memory_space=pltpu.VMEM)
    early, up, down = pl.pallas_call(
        functools.partial(pack_kernel, rows, groups),
        out_shape=[
            jax.ShapeDtypeStruct((EARLY * size + 32, size), jnp.bfloat16),
            jax.ShapeDtypeStruct((LATE * size, size), jnp.bfloat16),
            jax.ShapeDtypeStruct((LATE * size, size), jnp.bfloat16),
        ],
        in_specs=[smem, smem, smem, vmem],
        out_specs=[vmem, vmem, vmem],
        name="pack",
    )(table, density_pattern, filter_pattern, density.reshape(rows * slots, size, size))
    forward = [(i, (i + 1) % count) for i in range(count)]
    backward = [(j, i) for i, j in forward]
    late = lax.ppermute(up, "row", forward) + lax.ppermute(down, "row", backward)
    mine = jnp.concatenate([early, late], axis=0)
    gathered = lax.all_gather(mine, "col", axis=0, tiled=False)
    out = pl.pallas_call(
        functools.partial(multiply_kernel, rows, groups, early_tiles, late_tiles),
        out_shape=jax.ShapeDtypeStruct((rows * slots, size, size), jnp.bfloat16),
        in_specs=[smem, vmem],
        out_specs=vmem,
        scratch_shapes=[
            pltpu.VMEM((window * size, window * size), jnp.bfloat16),
            pltpu.VMEM((rows * size, window * size), jnp.bfloat16),
            pltpu.VMEM((window * size, 2 * size), jnp.bfloat16),
            pltpu.VMEM((groups * 32, size), jnp.float32),
        ],
        compiler_params=pltpu.CompilerParams(vmem_limit_bytes=60 * 1024 * 1024),
        name="multiply",
    )(filter_pattern, gathered)
    return out.reshape(rows, slots, size, size)


def solution(mesh):
    placed = (P("row", "col", None, None), P("row", "col"), P("row", "col"))
    return jax.shard_map(
        per_device,
        mesh=mesh,
        in_specs=placed,
        out_specs=P("row", "col", None, None),
        check_vma=False,
    )
```

```python
import functools

import jax
import jax.numpy as jnp
import numpy as np
from jax import lax
from jax.experimental import pallas as pl
from jax.experimental.pallas import tpu as pltpu
from jax.sharding import PartitionSpec as P

W = 8
EARLY = 8
AHEAD = 7
LATE = 6


def assign(rows, groups):
    size = rows + 2 * W
    items = [(u, v) for u in range(size) for v in range(u, min(size, u + W + 1))]

    def seats(pair):
        found = []
        for w, j in dict.fromkeys((pair, pair[::-1])):
            kind = 0 if W <= w < W + rows else 1
            found.append(((j % groups, kind), (w, j)))
        return sorted(found)

    room = {0: EARLY, 1: LATE}
    taken = {(m, kind): [] for m in range(groups) for kind in (0, 1)}

    def place(pair, seen):
        for seat, tile in seats(pair):
            if seat in seen:
                continue
            seen.add(seat)
            if len(taken[seat]) < room[seat[1]]:
                taken[seat].append((pair, tile))
                return True
            for index, (other, _) in enumerate(taken[seat]):
                if place(other, seen):
                    taken[seat][index] = (pair, tile)
                    return True
        return False

    for pair in items:
        if not place(pair, set()):
            raise ValueError("no room")
    early = [sorted(tile for _, tile in taken[m, 0]) for m in range(groups)]
    late = [sorted(tile for _, tile in taken[m, 1]) for m in range(groups)]
    return early, late


def slot_of(w, j, first):
    return (w - first) * 2 + (1 if j - w == W else 0)


def tables(early, late, rows, groups):
    out = np.full((groups, EARLY + 2 * LATE), -1, np.int32)
    for m in range(groups):
        for e, (w, j) in enumerate(early[m]):
            out[m, e] = slot_of(w, j, W)
        for e, (w, j) in enumerate(late[m]):
            if w < W:
                out[m, EARLY + e] = slot_of(w, j, W - rows)
            else:
                out[m, EARLY + LATE + e] = slot_of(w, j, W + rows)
    return out.reshape(-1)


def relative(row_index, col_index, rows, groups):
    return lax.rem(col_index - row_index * rows + W + groups * rows * 64, groups)


def masked_tile(pattern, density, slot):
    safe = jnp.maximum(slot, 0)
    used = (slot >= 0) & (pattern[lax.rem(safe, 2), safe // 2] == 1)
    tile = density[safe]
    return jnp.where(used, tile, jnp.zeros_like(tile))


def halo_kernel(rows, groups, table, pattern, density, up, down):
    size = density.shape[-1]
    width = EARLY + 2 * LATE
    r = lax.axis_index("row")
    c = lax.axis_index("col")
    after = relative(r + 1, c, rows, groups)
    before = relative(r + lax.axis_size("row") - 1, c, rows, groups)
    for e in range(LATE):
        place = pl.ds(e * size, size)
        up[place, :] = masked_tile(pattern, density, table[after * width + EARLY + e])
        down[place, :] = masked_tile(pattern, density, table[before * width + EARLY + LATE + e])


def own_kernel(rows, groups, table, pattern, keep, density, mine, extra, marks):
    size = density.shape[-1]
    width = EARLY + 2 * LATE
    own = relative(lax.axis_index("row"), lax.axis_index("col"), rows, groups)
    for e in range(EARLY):
        target, place = (mine, e) if e < AHEAD else (extra, e - AHEAD)
        target[pl.ds(place * size, size), :] = masked_tile(pattern, density, table[own * width + e])
    flags = jnp.zeros((32, size), jnp.float32)
    line = lax.broadcasted_iota(jnp.int32, (32, size), 0)
    for a in range(rows):
        for q in range(2):
            value = jnp.where(keep[q, a] == 1, 1.0, 0.0)
            flags = jnp.where(line == a * 2 + q, value, flags)
    marks[...] = flags.astype(jnp.bfloat16)


def multiply_kernel(rows, groups, early_tiles, late_tiles, keep, *refs):
    reach = groups // 4 - 1
    own_early, own_late = refs[:2]
    early_got, late_got = refs[2 : 2 + reach], refs[2 + reach : 2 + 2 * reach]
    far, out, pieces, dense, square, columns, flags, sems = refs[2 + 2 * reach :]
    size = out.shape[-1]
    window = rows + 2 * W
    r = lax.axis_index("row")
    c = lax.axis_index("col")
    m = relative(r, c, rows, groups)
    turn = lax.rem(c - m + groups, groups)
    pair = 2 * size
    half = W // 2
    supers = window // 2

    chips = groups // 2
    core = lax.rem(c, 2)
    first_lines = AHEAD * size
    last_lines = (EARLY - AHEAD + LATE) * size + 32
    copies = []
    for o in range(chips):
        for h in range(2):
            if o == 0:
                parts = [(own_early, h * first_lines), (own_late, h * last_lines)]
            elif o == chips // 2:
                base = h * (first_lines + last_lines)
                parts = [(far, base), (far, base + first_lines)]
            else:
                s = min(o, chips - o) - 1
                part = h + (2 if o < chips // 2 else 0)
                parts = [(early_got[s], part * first_lines), (late_got[s], part * last_lines)]
            place = 2 * o + h
            for k, (source, line) in enumerate(parts):
                start, count = ((0, first_lines), (first_lines, last_lines))[k]
                copy = pltpu.make_async_copy(
                    source.at[pl.ds(line, count), :], pieces.at[place, pl.ds(start, count), :], sems.at[place, k]
                )
                copy.start()
                copies.append(copy)

    nothing = jnp.zeros((size, size), jnp.bfloat16)
    for u in range(window):
        for v in range(window):
            if abs(u - v) > W and abs(u // 2 - v // 2) <= half:
                dense[pl.ds(u * size, size), pl.ds(v * size, size)] = nothing
    for copy in copies:
        copy.wait()
    for n in range(groups):
        place = lax.rem(turn + n + groups - (c - core), groups)
        for e, (w, j) in enumerate(early_tiles[n] + late_tiles[n]):
            line = (e if e < len(early_tiles[n]) else EARLY + e - len(early_tiles[n])) * size
            tile = pieces[place, pl.ds(line, size), :]
            dense[pl.ds(w * size, size), pl.ds(j * size, size)] = tile
            if w != j:
                dense[pl.ds(j * size, size), pl.ds(w * size, size)] = tile.T
        flags[pl.ds(n * 32, 32), :] = pieces[place, pl.ds((EARLY + LATE) * size, 32), :].astype(jnp.float32)

    first = pl.multiple_of(m * size, size)
    second = pl.multiple_of(jnp.minimum(m + groups, window - 1) * size, size)
    columns[...] = jnp.zeros_like(columns)
    for j, start, place in ((m, first, 0), (jnp.minimum(m + groups, window - 1), second, size)):
        for u in range(window):
            inside = (u - j <= W) & (j - u <= W)

            @pl.when(inside)
            def _():
                columns[pl.ds(u * size, size), pl.ds(place, size)] = dense[pl.ds(u * size, size), pl.ds(start, size)]

    for step in range(rows // 2):
        top = half + step
        line = top * pair
        for other in range(top - half, top + half + 1):
            if half <= other < top:
                continue
            low = max(top, other) - half
            high = min(top, other) + half + 1
            product = jnp.dot(
                dense[pl.ds(line, pair), pl.ds(low * pair, (high - low) * pair)],
                dense[pl.ds(low * pair, (high - low) * pair), pl.ds(other * pair, pair)],
                preferred_element_type=jnp.float32,
            )
            for x in range(2):
                for y in range(2):
                    a, k = 2 * step + x, 2 * other + y
                    d = k - (a + W)
                    if abs(d) > W:
                        tile = jnp.zeros((size, size), jnp.bfloat16)
                    else:
                        flag = flags[pl.ds((k % groups) * 32 + a * 2 + (1 if d == W else 0), 1), :]
                        tile = product[x * size : (x + 1) * size, y * size : (y + 1) * size]
                        tile = jnp.where(flag > 0.5, tile, 0.0).astype(jnp.bfloat16)
                    square[pl.ds(a * size, size), pl.ds(k * size, size)] = tile
                    if top < other < half + rows // 2:
                        square[pl.ds((k - W) * size, size), pl.ds((a + W) * size, size)] = tile.T
        low = (top - half) * pair
        deep = (2 * half + 1) * pair
        cubic = jnp.dot(
            square[pl.ds(step * pair, pair), pl.ds(low, deep)],
            columns[pl.ds(low, deep), :],
            preferred_element_type=jnp.float32,
        )
        for x in range(2):
            a = 2 * step + x
            upper = a <= m
            start = jnp.where(upper, first, second)
            start = pl.multiple_of(start, size)
            third = cubic[x * size : (x + 1) * size, :]
            chosen = jnp.where(upper, third[:, :size], third[:, size:])
            base = square[pl.ds(a * size, size), pl.ds(start, size)].astype(jnp.float32)
            value = 3.0 * base - 2.0 * chosen
            out[2 * a] = jnp.where(keep[0, a] == 1, value, 0.0).astype(out.dtype)
            there = (keep[1, a] == 1) & (a == m)
            base = square[pl.ds(a * size, size), pl.ds(second, size)].astype(jnp.float32)
            value = 3.0 * base - 2.0 * third[:, size:]
            out[2 * a + 1] = jnp.where(there, value, 0.0).astype(out.dtype)


def per_device(density, density_pattern, filter_pattern):
    rows, slots, size, _ = density.shape
    groups = lax.axis_size("col")
    count = lax.axis_size("row")
    early_tiles, late_tiles = assign(rows, groups)
    table = jnp.asarray(tables(early_tiles, late_tiles, rows, groups))
    window = rows + 2 * W
    smem = pl.BlockSpec(memory_space=pltpu.SMEM)
    vmem = pl.BlockSpec(memory_space=pltpu.VMEM)
    space = pl.BlockSpec(memory_space=pl.ANY)
    tiles = density.reshape(rows * slots, size, size)
    pattern, keep = density_pattern.T, filter_pattern.T
    lines = (EARLY + LATE) * size + 32
    part = jax.ShapeDtypeStruct((LATE * size, size), jnp.bfloat16)
    early, extra, marks = pl.pallas_call(
        functools.partial(own_kernel, rows, groups),
        out_shape=[
            jax.ShapeDtypeStruct((AHEAD * size, size), jnp.bfloat16),
            jax.ShapeDtypeStruct(((EARLY - AHEAD) * size, size), jnp.bfloat16),
            jax.ShapeDtypeStruct((32, size), jnp.bfloat16),
        ],
        in_specs=[smem, smem, smem, vmem],
        out_specs=[vmem, vmem, vmem],
        name="own_tiles",
    )(table, pattern, keep, tiles)
    forward = [(i, (i + 1) % count) for i in range(count)]
    backward = [(j, i) for i, j in forward]
    chips = groups // 2
    ring = [(2 * z, 2 * ((z + 1) % chips)) for z in range(chips)]
    ring += [(2 * z + 1, 2 * ((z - 1) % chips) + 1) for z in range(chips)]
    mates = [(i, i ^ 1) for i in range(groups)]
    both = [[2 * z, 2 * z + 1] for z in range(chips)]
    core = lax.rem(lax.axis_index("col"), 2)

    def with_mate(value):
        return lax.all_gather(value, "col", axis=0, tiled=True, axis_index_groups=both)

    def half(value):
        lines = value.shape[0] // 2
        return lax.dynamic_slice_in_dim(value, core * lines, lines, axis=0)

    own_early = with_mate(early)
    tiles, own_early = lax.optimization_barrier((tiles, own_early))
    up, down = pl.pallas_call(
        functools.partial(halo_kernel, rows, groups),
        out_shape=[part, part],
        in_specs=[smem, smem, vmem],
        out_specs=[vmem, vmem],
        name="halo_tiles",
    )(table, pattern, tiles)
    early_got = [lax.ppermute(own_early, "col", ring)]
    late = lax.ppermute(up, "row", forward) + lax.ppermute(down, "row", backward)
    late = jnp.concatenate([extra, late, marks], axis=0)
    late, early_got[0] = lax.optimization_barrier((late, early_got[0]))
    own_late = with_mate(late)
    late_got = [lax.ppermute(own_late, "col", ring)]
    for _ in range(chips // 2 - 2):
        early_got.append(lax.ppermute(early_got[-1], "col", ring))
        late_got.append(lax.ppermute(late_got[-1], "col", ring))
    early_last = lax.ppermute(half(early_got[-1]), "col", ring)
    late_last = lax.ppermute(half(late_got[-1]), "col", ring)
    early_got = [with_mate(value) for value in early_got]
    late_got = [with_mate(value) for value in late_got]
    far = with_mate(jnp.concatenate([early_last, late_last], axis=0))
    out = pl.pallas_call(
        functools.partial(multiply_kernel, rows, groups, early_tiles, late_tiles),
        out_shape=jax.ShapeDtypeStruct((rows * slots, size, size), jnp.bfloat16),
        in_specs=[smem] + [space] * (3 + len(early_got) + len(late_got)),
        out_specs=vmem,
        scratch_shapes=[
            pltpu.VMEM((groups, lines, size), jnp.bfloat16),
            pltpu.VMEM((window * size, window * size), jnp.bfloat16),
            pltpu.VMEM((rows * size, window * size), jnp.bfloat16),
            pltpu.VMEM((window * size, 2 * size), jnp.bfloat16),
            pltpu.VMEM((groups * 32, size), jnp.float32),
            pltpu.SemaphoreType.DMA((groups, 2)),
        ],
        compiler_params=pltpu.CompilerParams(vmem_limit_bytes=60 * 1024 * 1024),
        name="multiply",
    )(keep, own_early, own_late, *early_got, *late_got, far)
    return out.reshape(rows, slots, size, size)


def solution(mesh):
    placed = (P("row", "col", None, None), P("row", "col"), P("row", "col"))
    return jax.shard_map(
        per_device,
        mesh=mesh,
        in_specs=placed,
        out_specs=P("row", "col", None, None),
        check_vma=False,
    )
```

```python
import functools

import jax
import jax.numpy as jnp
import numpy as np
from jax import lax
from jax.experimental import pallas as pl
from jax.experimental.pallas import tpu as pltpu
from jax.sharding import PartitionSpec as P

W = 8
EARLY = 8
AHEAD = 7
LATE = 6


def assign(rows, groups):
    size = rows + 2 * W
    items = [(u, v) for u in range(size) for v in range(u, min(size, u + W + 1))]

    def seats(pair):
        found = []
        for w, j in dict.fromkeys((pair, pair[::-1])):
            kind = 0 if W <= w < W + rows else 1
            found.append(((j % groups, kind), (w, j)))
        return sorted(found)

    room = {0: EARLY, 1: LATE}
    taken = {(m, kind): [] for m in range(groups) for kind in (0, 1)}

    def place(pair, seen):
        for seat, tile in seats(pair):
            if seat in seen:
                continue
            seen.add(seat)
            if len(taken[seat]) < room[seat[1]]:
                taken[seat].append((pair, tile))
                return True
            for index, (other, _) in enumerate(taken[seat]):
                if place(other, seen):
                    taken[seat][index] = (pair, tile)
                    return True
        return False

    for pair in items:
        if not place(pair, set()):
            raise ValueError("no room")
    early = [sorted(tile for _, tile in taken[m, 0]) for m in range(groups)]
    late = [sorted(tile for _, tile in taken[m, 1]) for m in range(groups)]
    return early, late


def slot_of(w, j, first):
    return (w - first) * 2 + (1 if j - w == W else 0)


def tables(early, late, rows, groups):
    out = np.full((groups, EARLY + 2 * LATE), -1, np.int32)
    for m in range(groups):
        for e, (w, j) in enumerate(early[m]):
            out[m, e] = slot_of(w, j, W)
        for e, (w, j) in enumerate(late[m]):
            if w < W:
                out[m, EARLY + e] = slot_of(w, j, W - rows)
            else:
                out[m, EARLY + LATE + e] = slot_of(w, j, W + rows)
    return out.reshape(-1)


def relative(row_index, col_index, rows, groups):
    return lax.rem(col_index - row_index * rows + W + groups * rows * 64, groups)


def masked_tile(pattern, density, slot):
    safe = jnp.maximum(slot, 0)
    used = (slot >= 0) & (pattern[lax.rem(safe, 2), safe // 2] == 1)
    tile = density[safe]
    return jnp.where(used, tile, jnp.zeros_like(tile))


def halo_kernel(rows, groups, table, pattern, density, up, down):
    size = density.shape[-1]
    width = EARLY + 2 * LATE
    r = lax.axis_index("row")
    c = lax.axis_index("col")
    after = relative(r + 1, c, rows, groups)
    before = relative(r + lax.axis_size("row") - 1, c, rows, groups)
    for e in range(LATE):
        place = pl.ds(e * size, size)
        up[place, :] = masked_tile(pattern, density, table[after * width + EARLY + e])
        down[place, :] = masked_tile(pattern, density, table[before * width + EARLY + LATE + e])


def own_kernel(rows, groups, table, pattern, keep, density, mine, extra, marks):
    size = density.shape[-1]
    width = EARLY + 2 * LATE
    own = relative(lax.axis_index("row"), lax.axis_index("col"), rows, groups)
    for e in range(EARLY):
        target, place = (mine, e) if e < AHEAD else (extra, e - AHEAD)
        target[pl.ds(place * size, size), :] = masked_tile(pattern, density, table[own * width + e])
    flags = jnp.zeros((32, size), jnp.float32)
    line = lax.broadcasted_iota(jnp.int32, (32, size), 0)
    for a in range(rows):
        for q in range(2):
            value = jnp.where(keep[q, a] == 1, 1.0, 0.0)
            flags = jnp.where(line == a * 2 + q, value, flags)
    marks[...] = flags.astype(jnp.bfloat16)


def multiply_kernel(rows, groups, early_tiles, late_tiles, keep, *refs):
    reach = groups // 4 - 1
    own_early, own_late = refs[:2]
    early_got, late_got = refs[2 : 2 + reach], refs[2 + reach : 2 + 2 * reach]
    far_early, far_late, out, pieces, dense, square, columns, flags, sems = refs[2 + 2 * reach :]
    size = out.shape[-1]
    window = rows + 2 * W
    r = lax.axis_index("row")
    c = lax.axis_index("col")
    m = relative(r, c, rows, groups)
    turn = lax.rem(c - m + groups, groups)
    pair = 2 * size
    half = W // 2

    chips = groups // 2
    core = lax.rem(c, 2)
    first_lines = AHEAD * size
    last_lines = (EARLY - AHEAD + LATE) * size + 32
    copies = []
    for o in range(chips):
        for h in range(2):
            if o == 0:
                parts = [(own_early, h * first_lines), (own_late, h * last_lines)]
            elif o == chips // 2:
                parts = [(far_early, h * first_lines), (far_late, h * last_lines)]
            else:
                s = min(o, chips - o) - 1
                part = h + (2 if o < chips // 2 else 0)
                parts = [(early_got[s], part * first_lines), (late_got[s], part * last_lines)]
            place = 2 * o + h
            for k, (source, line) in enumerate(parts):
                start, count = ((0, first_lines), (first_lines, last_lines))[k]
                copy = pltpu.make_async_copy(
                    source.at[pl.ds(line, count), :], pieces.at[place, pl.ds(start, count), :], sems.at[place, k]
                )
                copy.start()
                copies.append(copy)

    nothing = jnp.zeros((size, size), jnp.bfloat16)
    for u in range(window):
        for v in range(window):
            if abs(u - v) > W and abs(u // 2 - v // 2) <= half:
                dense[pl.ds(u * size, size), pl.ds(v * size, size)] = nothing
    for copy in copies:
        copy.wait()
    for n in range(groups):
        place = lax.rem(turn + n + groups - (c - core), groups)
        for e, (w, j) in enumerate(early_tiles[n] + late_tiles[n]):
            line = (e if e < len(early_tiles[n]) else EARLY + e - len(early_tiles[n])) * size
            tile = pieces[place, pl.ds(line, size), :]
            dense[pl.ds(w * size, size), pl.ds(j * size, size)] = tile
            if w != j:
                dense[pl.ds(j * size, size), pl.ds(w * size, size)] = tile.T
        flags[pl.ds(n * 32, 32), :] = pieces[place, pl.ds((EARLY + LATE) * size, 32), :].astype(jnp.float32)

    first = pl.multiple_of(m * size, size)
    second = pl.multiple_of(jnp.minimum(m + groups, window - 1) * size, size)
    columns[...] = jnp.zeros_like(columns)
    for j, start, place in ((m, first, 0), (jnp.minimum(m + groups, window - 1), second, size)):
        for u in range(window):
            inside = (u - j <= W) & (j - u <= W)

            @pl.when(inside)
            def _():
                columns[pl.ds(u * size, size), pl.ds(place, size)] = dense[pl.ds(u * size, size), pl.ds(start, size)]

    for step in range(rows // 2):
        top = half + step
        line = top * pair
        for other in range(top - half, top + half + 1):
            if half <= other < top:
                continue
            low = max(top, other) - half
            high = min(top, other) + half + 1
            product = jnp.dot(
                dense[pl.ds(line, pair), pl.ds(low * pair, (high - low) * pair)],
                dense[pl.ds(low * pair, (high - low) * pair), pl.ds(other * pair, pair)],
                preferred_element_type=jnp.float32,
            )
            for x in range(2):
                for y in range(2):
                    a, k = 2 * step + x, 2 * other + y
                    d = k - (a + W)
                    if abs(d) > W:
                        tile = jnp.zeros((size, size), jnp.bfloat16)
                    else:
                        flag = flags[pl.ds((k % groups) * 32 + a * 2 + (1 if d == W else 0), 1), :]
                        tile = product[x * size : (x + 1) * size, y * size : (y + 1) * size]
                        tile = jnp.where(flag > 0.5, tile, 0.0).astype(jnp.bfloat16)
                    square[pl.ds(a * size, size), pl.ds(k * size, size)] = tile
                    if top < other < half + rows // 2:
                        square[pl.ds((k - W) * size, size), pl.ds((a + W) * size, size)] = tile.T
        low = (top - half) * pair
        deep = (2 * half + 1) * pair
        cubic = jnp.dot(
            square[pl.ds(step * pair, pair), pl.ds(low, deep)],
            columns[pl.ds(low, deep), :],
            preferred_element_type=jnp.float32,
        )
        for x in range(2):
            a = 2 * step + x
            upper = a <= m
            start = jnp.where(upper, first, second)
            start = pl.multiple_of(start, size)
            third = cubic[x * size : (x + 1) * size, :]
            chosen = jnp.where(upper, third[:, :size], third[:, size:])
            base = square[pl.ds(a * size, size), pl.ds(start, size)].astype(jnp.float32)
            value = 3.0 * base - 2.0 * chosen
            out[2 * a] = jnp.where(keep[0, a] == 1, value, 0.0).astype(out.dtype)
            there = (keep[1, a] == 1) & (a == m)
            base = square[pl.ds(a * size, size), pl.ds(second, size)].astype(jnp.float32)
            value = 3.0 * base - 2.0 * third[:, size:]
            out[2 * a + 1] = jnp.where(there, value, 0.0).astype(out.dtype)


def per_device(density, density_pattern, filter_pattern):
    rows, slots, size, _ = density.shape
    groups = lax.axis_size("col")
    count = lax.axis_size("row")
    early_tiles, late_tiles = assign(rows, groups)
    table = jnp.asarray(tables(early_tiles, late_tiles, rows, groups))
    window = rows + 2 * W
    smem = pl.BlockSpec(memory_space=pltpu.SMEM)
    vmem = pl.BlockSpec(memory_space=pltpu.VMEM)
    space = pl.BlockSpec(memory_space=pl.ANY)
    tiles = density.reshape(rows * slots, size, size)
    pattern, keep = density_pattern.T, filter_pattern.T
    lines = (EARLY + LATE) * size + 32
    part = jax.ShapeDtypeStruct((LATE * size, size), jnp.bfloat16)
    early, extra, marks = pl.pallas_call(
        functools.partial(own_kernel, rows, groups),
        out_shape=[
            jax.ShapeDtypeStruct((AHEAD * size, size), jnp.bfloat16),
            jax.ShapeDtypeStruct(((EARLY - AHEAD) * size, size), jnp.bfloat16),
            jax.ShapeDtypeStruct((32, size), jnp.bfloat16),
        ],
        in_specs=[smem, smem, smem, vmem],
        out_specs=[vmem, vmem, vmem],
        name="own_tiles",
    )(table, pattern, keep, tiles)
    forward = [(i, (i + 1) % count) for i in range(count)]
    backward = [(j, i) for i, j in forward]
    chips = groups // 2
    ring = [(2 * z, 2 * ((z + 1) % chips)) for z in range(chips)]
    ring += [(2 * z + 1, 2 * ((z - 1) % chips) + 1) for z in range(chips)]
    mates = [(i, i ^ 1) for i in range(groups)]
    both = [[2 * z, 2 * z + 1] for z in range(chips)]
    core = lax.rem(lax.axis_index("col"), 2)

    def with_mate(value):
        return lax.all_gather(value, "col", axis=0, tiled=True, axis_index_groups=both)

    def half(value):
        lines = value.shape[0] // 2
        return lax.dynamic_slice_in_dim(value, core * lines, lines, axis=0)

    own_early = with_mate(early)
    tiles, own_early = lax.optimization_barrier((tiles, own_early))
    up, down = pl.pallas_call(
        functools.partial(halo_kernel, rows, groups),
        out_shape=[part, part],
        in_specs=[smem, smem, vmem],
        out_specs=[vmem, vmem],
        name="halo_tiles",
    )(table, pattern, tiles)
    early_got = [lax.ppermute(own_early, "col", ring)]
    late = lax.ppermute(up, "row", forward) + lax.ppermute(down, "row", backward)
    late = jnp.concatenate([extra, late, marks], axis=0)
    late, early_got[0] = lax.optimization_barrier((late, early_got[0]))
    own_late = with_mate(late)
    late_got = [lax.ppermute(own_late, "col", ring)]
    for _ in range(chips // 2 - 2):
        early_got.append(lax.ppermute(early_got[-1], "col", ring))
        late_got.append(lax.ppermute(late_got[-1], "col", ring))
    early_last = lax.ppermute(half(early_got[-1]), "col", ring)
    late_last = lax.ppermute(half(late_got[-1]), "col", ring)
    early_got = [with_mate(value) for value in early_got]
    late_got = [with_mate(value) for value in late_got]
    far = [with_mate(early_last), with_mate(late_last)]
    out = pl.pallas_call(
        functools.partial(multiply_kernel, rows, groups, early_tiles, late_tiles),
        out_shape=jax.ShapeDtypeStruct((rows * slots, size, size), jnp.bfloat16),
        in_specs=[smem] + [space] * (4 + len(early_got) + len(late_got)),
        out_specs=vmem,
        scratch_shapes=[
            pltpu.VMEM((groups, lines, size), jnp.bfloat16),
            pltpu.VMEM((window * size, window * size), jnp.bfloat16),
            pltpu.VMEM((rows * size, window * size), jnp.bfloat16),
            pltpu.VMEM((window * size, 2 * size), jnp.bfloat16),
            pltpu.VMEM((groups * 32, size), jnp.float32),
            pltpu.SemaphoreType.DMA((groups, 2)),
        ],
        compiler_params=pltpu.CompilerParams(vmem_limit_bytes=60 * 1024 * 1024),
        name="multiply",
    )(keep, own_early, own_late, *early_got, *late_got, *far)
    return out.reshape(rows, slots, size, size)


def solution(mesh):
    placed = (P("row", "col", None, None), P("row", "col"), P("row", "col"))
    return jax.shard_map(
        per_device,
        mesh=mesh,
        in_specs=placed,
        out_specs=P("row", "col", None, None),
        check_vma=False,
    )
```
